32 devices in a mesh: row: 16 (over z, x, core), col: 2 (over y).
Axes of the slice: x: 2, y: 2, z: 4, core: 2. Of those that a mesh axis runs over, the one named last changes fastest.
Arguments:
- corr: float32 [2, 8192, 8192], P(None, 'row', 'col'), may hold values from -6 to 6
- slope_prev: float32 [2, 8192, 8192], P(None, 'row', 'col'), may hold values from -6 to 6
- kappa: float32 [8192], replicated, may hold values from 0.05 to 0.2
- detuning: float32 [8192], replicated, may hold values from -1 to 1
- pump: float32 [8192], replicated, may hold values from 0.5 to 2
- round_trip: float32 [2], replicated, may hold values from -0.6 to 0.6
Outputs:
- slope: float32 [2, 8192, 8192], P(None, 'row', 'col')
The draws below stay inside these ranges and needn't reach their ends.
All inputs are finite; a program needn't handle non-finite values.
Results may differ from the reference program's by a relative error of at most 0.00005.
Values sent between devices are 32-bit elements; how exact they have to be, the bound alone decides.
A program may use at most 256 MiB of HBM per device.

```python
import math
import jax
import jax.numpy as jnp

N = 8192


def shard_levels(stream_key, shape, shards, smallest, top_value):
    level, own = 1.0, jax.random.fold_in(stream_key, 6)
    for position, parts in shards:
        heights = jnp.exp(jax.random.uniform(jax.random.fold_in(own, position), (parts,), jnp.float32, smallest / len(shards), top_value / len(shards)))
        level = level * jnp.repeat(heights, shape[position] // parts).reshape([-1 if axis == position else 1 for axis in range(len(shape))])
    return level


def noise(stream_key, dims, spread, limit, cuts=(), kind=jnp.bfloat16):
    values = spread * jax.random.normal(stream_key, dims, jnp.float32)
    if cuts:
        values = values * shard_levels(stream_key, dims, cuts, -0.22, 0.18)
    return jnp.clip(values, -limit, limit).astype(kind)


def setup_inputs(seed: int = 0) -> dict:
    key_list = jax.random.split(jax.random.key(seed), 7)
    return {
        "corr": noise(key_list[0], (2, N, N), 1.0, 6.0, ((1, 16), (2, 2)), jnp.float32),
        "slope_prev": noise(key_list[1], (2, N, N), 1.0, 6.0, ((1, 16), (2, 2)), jnp.float32),
        "kappa": jnp.clip(jnp.exp(jax.random.uniform(key_list[2], (N,), jnp.float32, math.log(0.05), math.log(0.2))), 0.05, 0.2),
        "detuning": jnp.clip(jax.random.uniform(key_list[3], (N,), jnp.float32, -1.0, 1.0), -1.0, 1.0),
        "pump": jnp.clip(jax.random.uniform(key_list[4], (N,), jnp.float32, 0.5, 2.0), 0.5, 2.0),
        "round_trip": jnp.clip(jax.random.uniform(key_list[5], (2,), jnp.float32, -0.6, 0.6), -0.6, 0.6),
    }


def reference(corr, slope_prev, kappa, detuning, pump, round_trip):
    section = corr + 0.25 * slope_prev
    rho_re = round_trip[0]
    rho_im = round_trip[1]
    upper = section * kappa[None, :, None]
    inclusive = jnp.cumsum(upper, axis=1)
    before = inclusive - upper
    after = inclusive[:, -1:, :] - inclusive
    turned = jnp.stack([rho_re * after[0] - rho_im * after[1], rho_re * after[1] + rho_im * after[0]])
    field_left = -kappa[None, :, None] * (before + 0.5 * upper + turned)
    weighted = section * kappa[None, None, :]
    inclusive = jnp.cumsum(weighted, axis=2)
    before = inclusive - weighted
    after = inclusive[:, :, -1:] - inclusive
    turned = jnp.stack([rho_re * after[0] + rho_im * after[1], rho_re * after[1] - rho_im * after[0]])
    field_right = -kappa[None, None, :] * (before + 0.5 * weighted + turned)
    gap = detuning[None, :] - detuning[:, None]
    spin = jnp.stack([-gap * section[1], gap * section[0]])
    slope = field_left + field_right + spin
    index = jnp.arange(kappa.shape[0], dtype=jnp.int32)
    slope = slope.at[0, index, index].add(pump)
    return slope
```

```python
import functools

import jax
import jax.numpy as jnp
from jax import lax
from jax.experimental import pallas as pl
from jax.experimental.pallas import tpu as pltpu
from jax.sharding import PartitionSpec as P

WIDTH = 256
SLAB = 32
MESH = pl.DeviceIdType.MESH
VMEM = pl.BlockSpec(memory_space=pltpu.VMEM)
SMEM = pl.BlockSpec(memory_space=pltpu.SMEM)


def split(value):
    high = value.astype(jnp.bfloat16)
    return high, (value - high.astype(jnp.float32)).astype(jnp.bfloat16)


def local_kernel(corr, prev, kappa, detuning, pump, trip, out, row_sums, col_sums,
                 tables, pump_col, u_parts, w_parts, left, right, carry, sums):
    rows = out.shape[1]
    cols = out.shape[2]
    blocks = rows // WIDTH
    step = pl.program_id(0)
    row_start = pl.multiple_of(lax.axis_index("row") * rows, WIDTH)
    col_start = pl.multiple_of(lax.axis_index("col") * cols + step * WIDTH, WIDTH)
    rho_re = trip[0]
    rho_im = trip[1]

    @pl.when(step == 0)
    def _():
        mine = pl.ds(row_start, rows)
        kr = kappa[:, mine]
        stacked = jnp.concatenate(
            [kr, (rho_re - 1.0) * kr, rho_im * kr, (0.5 * rho_re) * kr * kr,
             detuning[:, mine] - (0.5 * rho_im) * kr * kr, pump[:, mine], kr, kr], axis=0)
        columns = jnp.transpose(stacked)
        for n in range(5):
            tables[n] = jnp.broadcast_to(columns[:, n:n + 1], (rows, WIDTH // 2))
        pump_col[...] = jnp.broadcast_to(columns[:, 5:6], (rows, WIDTH // 2))
        carry[...] = jnp.zeros_like(carry)

    here = pl.ds(pl.multiple_of(step * WIDTH, WIDTH), WIDTH)
    kc = kappa[:, pl.ds(col_start, WIDTH)]
    br = (rho_re - 1.0) * kc
    bi = -rho_im * kc
    pk = (0.5 * rho_re) * kc * kc
    ak = detuning[:, pl.ds(col_start, WIDTH)] - (0.5 * rho_im) * kc * kc

    def wide(value):
        return jnp.concatenate([value, value], axis=1)

    above = lax.broadcasted_iota(jnp.int32, (WIDTH, WIDTH), 0)
    beside = lax.broadcasted_iota(jnp.int32, (WIDTH, WIDTH), 1)
    half = jnp.where(above == beside, 0.5, 0.0)
    lower = jnp.where(above > beside, 1.0, half).astype(jnp.bfloat16)
    upper = jnp.where(above < beside, 1.0, half).astype(jnp.bfloat16)
    lower2 = jnp.concatenate([lower, lower], axis=1)
    upper2 = jnp.concatenate([upper, upper], axis=0)

    before = [jnp.zeros((1, WIDTH), jnp.float32)] * 2
    for b in range(blocks):
        def prepare(n, acc):
            low = pl.multiple_of(n * SLAB, SLAB)
            at = pl.ds(pl.multiple_of(b * WIDTH + low, SLAB), SLAB)
            kr = wide(tables[0, at, :])
            new = []
            for p in range(2):
                s = corr[p, at, :] + 0.25 * prev[p, at, :]
                out[p, at, here] = s
                u = s * kr
                high, rest = split(u)
                u_parts[pl.ds(low, SLAB), p * WIDTH:(p + 1) * WIDTH] = high
                u_parts[pl.ds(pl.multiple_of(WIDTH + low, SLAB), SLAB), p * WIDTH:(p + 1) * WIDTH] = rest
                high, rest = split(s * kc)
                w_parts[p, pl.ds(low, SLAB), :WIDTH] = high
                w_parts[p, pl.ds(low, SLAB), WIDTH:] = rest
                new.append(acc[p] + jnp.sum(u.reshape(SLAB // 8, 8, WIDTH), axis=0))
            return tuple(new)

        zero = jnp.zeros((8, WIDTH), jnp.float32)
        acc = lax.fori_loop(0, WIDTH // SLAB, prepare, (zero, zero), unroll=2)

        left[...] = jnp.dot(lower2, u_parts[...], preferred_element_type=jnp.float32)
        for p in range(2):
            right[p] = jnp.dot(w_parts[p], upper2, preferred_element_type=jnp.float32)

        def combine(n, token):
            low = pl.multiple_of(n * SLAB, SLAB)
            at = pl.ds(pl.multiple_of(b * WIDTH + low, SLAB), SLAB)
            near = pl.ds(low, SLAB)
            ar, ai, pi, di = [wide(tables[t, at, :]) for t in range(1, 5)]
            s = [out[p, at, here] for p in range(2)]
            x = [left[near, p * WIDTH:(p + 1) * WIDTH] for p in range(2)]
            if b:
                x = [x[p] + before[p] for p in range(2)]
            y = []
            for p in range(2):
                held = carry[p, at, :]
                piece = right[p, near, :] + wide(held)
                y.append(piece)
                last = piece[:, WIDTH - 1:] + (0.5 * kc[:, WIDTH - 1:]) * s[p][:, WIDTH - 1:]
                carry[p, at, :] = jnp.broadcast_to(last, held.shape)
            cr = pi + pk
            ci = ak - di
            out[0, at, here] = (cr * s[0] - ci * s[1]) + (ar * x[0] - ai * x[1]) + (br * y[0] - bi * y[1])
            out[1, at, here] = (cr * s[1] + ci * s[0]) + (ar * x[1] + ai * x[0]) + (br * y[1] + bi * y[0])
            return token

        lax.fori_loop(0, WIDTH // SLAB, combine, 0, unroll=2)
        before = [before[p] + jnp.sum(acc[p], axis=0, keepdims=True) for p in range(2)]

    offset = col_start - row_start

    @pl.when(jnp.logical_and(offset >= 0, offset < rows))
    def _():
        at = pl.ds(pl.multiple_of(offset, WIDTH), WIDTH)
        out[0, at, here] += jnp.where(above == beside, wide(pump_col[at, :]), 0.0)

    sums[:, here] = jnp.concatenate(before, axis=0)

    @pl.when(step == pl.num_programs(0) - 1)
    def _():
        count, _, width = row_sums.shape
        for n in range(count):
            row_sums[n] = sums[:, n * width:(n + 1) * width]
        for p in range(2):
            col_sums[8 * p:8 * p + 8, :] = jnp.transpose(carry[p])[:8, :]


def prefix_pair(value, total, rho_re, rho_im):
    re = value[0:1] + rho_re * (total[0:1] - value[0:1]) - rho_im * (total[1:2] - value[1:2])
    im = value[1:2] + rho_re * (total[1:2] - value[1:2]) + rho_im * (total[0:1] - value[0:1])
    return re, im


def exchange_kernel(row_sums, col_sums, trip, row_fix, col_fix,
                    got, back, ready, cols_got, send, recv, send_back, recv_back, send_col, recv_col):
    count = row_sums.shape[0]
    col_count = cols_got.shape[0]
    me = lax.axis_index("row")
    my_col = lax.axis_index("col")
    rho_re = trip[0]
    rho_im = trip[1]

    def row_peer(j):
        return (lax.rem(me + j, count), my_col)

    def col_peer(j):
        return (me, lax.rem(my_col + j, col_count))

    barrier = pltpu.get_barrier_semaphore()
    for j in range(1, count):
        pl.semaphore_signal(barrier, inc=1, device_id=row_peer(j), device_id_type=MESH)
    for j in range(1, col_count):
        pl.semaphore_signal(barrier, inc=1, device_id=col_peer(j), device_id_type=MESH)
    pl.semaphore_wait(barrier, count + col_count - 2)

    first, second, across = [], [], []
    for j in range(1, count):
        first.append(pltpu.make_async_remote_copy(
            src_ref=row_sums.at[lax.rem(me + j, count)], dst_ref=got.at[j],
            send_sem=send.at[j], recv_sem=recv.at[j], device_id=row_peer(j), device_id_type=MESH))
        first[-1].start()
    for j in range(1, col_count):
        across.append(pltpu.make_async_remote_copy(
            src_ref=col_sums, dst_ref=cols_got.at[j],
            send_sem=send_col.at[j], recv_sem=recv_col.at[j], device_id=col_peer(j), device_id_type=MESH))
        across[-1].start()
    got[0] = row_sums[me]
    cols_got[0] = col_sums[...]
    for copy in first:
        copy.wait_recv()
    running = jnp.zeros(got.shape[1:], jnp.float32)
    held = []
    for n in range(count):
        held.append(running)
        running = running + got[lax.rem(me - n + count, count)]
    for n in range(count):
        re, im = prefix_pair(held[n], running, rho_re, rho_im)
        ready[lax.rem(n - me + count, count)] = jnp.concatenate([re, im], axis=0)
    for j in range(1, count):
        second.append(pltpu.make_async_remote_copy(
            src_ref=ready.at[j], dst_ref=back.at[j],
            send_sem=send_back.at[j], recv_sem=recv_back.at[j], device_id=row_peer(j), device_id_type=MESH))
        second[-1].start()
    for copy in across:
        copy.wait_recv()
    running = jnp.zeros(col_sums.shape, jnp.float32)
    mine = running
    for n in range(col_count):
        piece = cols_got[lax.rem(my_col - n + col_count, col_count)]
        mine = mine + jnp.where(n < my_col, piece, 0.0)
        running = running + piece
    rest = running - mine
    col_fix[0:8, :] = mine[0:8] + rho_re * rest[0:8] + rho_im * rest[8:16]
    col_fix[8:16, :] = mine[8:16] + rho_re * rest[8:16] - rho_im * rest[0:8]
    for copy in second:
        copy.wait_recv()
    row_fix[me] = ready[0]
    for j in range(1, count):
        row_fix[lax.rem(me - j + count, count)] = back[j]
    for copy in first + across + second:
        copy.wait_send()


def finish_kernel(local, row_fix, col_fix, kappa, out, tables, across):
    step = pl.program_id(0)
    rows = local.shape[1]
    cols = local.shape[2]
    slab = out.shape[1]

    @pl.when(step == 0)
    def _():
        mine = pl.ds(pl.multiple_of(lax.axis_index("row") * rows, WIDTH), rows)
        stacked = jnp.concatenate([col_fix[0:1, :], col_fix[8:9, :], kappa[:, mine]] + [col_fix[0:5, :]], axis=0)
        columns = jnp.transpose(stacked)
        for n in range(3):
            tables[n] = jnp.broadcast_to(columns[:, n:n + 1], tables.shape[1:])
        count = row_fix.shape[0]
        across[...] = jnp.concatenate([row_fix[n] for n in range(count)], axis=1)

    at = pl.ds(pl.multiple_of(step * slab, slab), slab)
    col_start = lax.axis_index("col") * cols
    kr = tables[2, at, :]
    fix = [tables[p, at, :] for p in range(2)]
    for n in range(cols // 128):
        here = slice(n * 128, (n + 1) * 128)
        kc = kappa[:, pl.ds(pl.multiple_of(col_start + n * 128, 128), 128)]
        for p in range(2):
            out[p, :, here] = local[p, at, here] - kr * across[p:p + 1, here] - kc * fix[p]


def shards(row_count, col_count, corr, slope_prev, kappa, detuning, pump, round_trip):
    _, rows, cols = corr.shape
    width = cols // row_count
    kappa, detuning, pump = [v.reshape(1, -1) for v in (kappa, detuning, pump)]
    f32 = jnp.float32
    block = pl.BlockSpec((2, rows, WIDTH), lambda c: (0, 0, c))
    local, row_sums, col_sums = pl.pallas_call(
        local_kernel,
        grid=(cols // WIDTH,),
        out_shape=(
            pltpu.VMEM((2, rows, cols), f32),
            jax.ShapeDtypeStruct((row_count, 2, width), f32),
            jax.ShapeDtypeStruct((16, rows), f32),
        ),
        in_specs=[block, block, VMEM, VMEM, VMEM, SMEM],
        out_specs=(VMEM, VMEM, VMEM),
        scratch_shapes=[
            pltpu.VMEM((5, rows, WIDTH // 2), f32),
            pltpu.VMEM((rows, WIDTH // 2), f32),
            pltpu.VMEM((2 * WIDTH, 2 * WIDTH), jnp.bfloat16),
            pltpu.VMEM((2, WIDTH, 2 * WIDTH), jnp.bfloat16),
            pltpu.VMEM((WIDTH, 2 * WIDTH), f32),
            pltpu.VMEM((2, WIDTH, WIDTH), f32),
            pltpu.VMEM((2, rows, WIDTH // 2), f32),
            pltpu.VMEM((2, cols), f32),
        ],
        compiler_params=pltpu.CompilerParams(vmem_limit_bytes=34 << 20),
        name="local_part",
    )(corr, slope_prev, kappa, detuning, pump, round_trip)
    piece = (row_count, 2, width)
    row_fix, col_fix = pl.pallas_call(
        exchange_kernel,
        out_shape=(jax.ShapeDtypeStruct(piece, f32), jax.ShapeDtypeStruct((16, rows), f32)),
        in_specs=[VMEM, VMEM, SMEM],
        out_specs=(VMEM, VMEM),
        scratch_shapes=[
            pltpu.VMEM(piece, f32),
            pltpu.VMEM(piece, f32),
            pltpu.VMEM(piece, f32),
            pltpu.VMEM((col_count, 16, rows), f32),
        ] + [pltpu.SemaphoreType.DMA((row_count,))] * 4 + [pltpu.SemaphoreType.DMA((col_count,))] * 2,
        compiler_params=pltpu.CompilerParams(
            collective_id=0, has_side_effects=True, vmem_limit_bytes=6 << 20),
        name="exchange_sums",
    )(row_sums, col_sums, round_trip)
    slab = 32
    return pl.pallas_call(
        finish_kernel,
        grid=(rows // slab,),
        out_shape=jax.ShapeDtypeStruct((2, rows, cols), f32),
        in_specs=[VMEM, VMEM, VMEM, VMEM],
        out_specs=pl.BlockSpec((2, slab, cols), lambda r: (0, r, 0)),
        scratch_shapes=[pltpu.VMEM((3, rows, 128), f32), pltpu.VMEM((2, cols), f32)],
        compiler_params=pltpu.CompilerParams(vmem_limit_bytes=10 << 20),
        name="finish",
    )(local, row_fix, col_fix, kappa)


def solution(mesh):
    placed = (P(None, "row", "col"), P(None, "row", "col"), P(), P(), P(), P())
    body = functools.partial(shards, mesh.shape["row"], mesh.shape["col"])
    return jax.shard_map(
        body, mesh=mesh, in_specs=placed, out_specs=P(None, "row", "col"), check_vma=False
    )
```

```python
import functools

import jax
import jax.numpy as jnp
from jax import lax
from jax.experimental import pallas as pl
from jax.experimental.pallas import tpu as pltpu
from jax.sharding import PartitionSpec as P

WIDTH = 256
TRI = 128
SLAB = 16
MESH = pl.DeviceIdType.MESH
VMEM = pl.BlockSpec(memory_space=pltpu.VMEM)
SMEM = pl.BlockSpec(memory_space=pltpu.SMEM)


def split(value):
    high = value.astype(jnp.bfloat16)
    return high, (value - high.astype(jnp.float32)).astype(jnp.bfloat16)


def local_kernel(corr, prev, kappa, detuning, pump, trip, out, row_sums, col_sums,
                 tables, pump_col, u_parts, w_parts, left, right, carry, sums, lower2, upper2, section):
    rows = out.shape[1]
    cols = out.shape[2]
    blocks = rows // TRI
    step = pl.program_id(0)
    row_start = pl.multiple_of(lax.axis_index("row") * rows, WIDTH)
    col_start = pl.multiple_of(lax.axis_index("col") * cols + step * WIDTH, WIDTH)
    rho_re = trip[0]
    rho_im = trip[1]

    @pl.when(step == 0)
    def _():
        mine = pl.ds(row_start, rows)
        kr = kappa[:, mine]
        stacked = jnp.concatenate(
            [kr, (rho_re - 1.0) * kr, rho_im * kr, (0.5 * rho_re) * kr * kr,
             detuning[:, mine] - (0.5 * rho_im) * kr * kr, pump[:, mine], kr, kr], axis=0)
        columns = jnp.transpose(stacked)
        for n in range(5):
            tables[n] = jnp.broadcast_to(columns[:, n:n + 1], (rows, WIDTH // 2))
        pump_col[...] = jnp.broadcast_to(columns[:, 5:6], (rows, WIDTH // 2))
        carry[...] = jnp.zeros_like(carry)
        above = lax.broadcasted_iota(jnp.int32, (TRI, TRI), 0)
        beside = lax.broadcasted_iota(jnp.int32, (TRI, TRI), 1)
        half = jnp.where(above == beside, 0.5, 0.0)
        lower = jnp.where(above > beside, 1.0, half).astype(jnp.bfloat16)
        upper = jnp.where(above < beside, 1.0, half).astype(jnp.bfloat16)
        full = jnp.ones((2 * TRI, TRI), jnp.bfloat16)
        lower2[...] = jnp.concatenate([lower, lower], axis=1)
        upper2[...] = jnp.concatenate([jnp.concatenate([upper, upper], axis=0), full], axis=1)

    here = pl.ds(pl.multiple_of(step * WIDTH, WIDTH), WIDTH)
    kc = kappa[:, pl.ds(col_start, WIDTH)]
    br = (rho_re - 1.0) * kc
    bi = -rho_im * kc
    pk = (0.5 * rho_re) * kc * kc
    ak = detuning[:, pl.ds(col_start, WIDTH)] - (0.5 * rho_im) * kc * kc

    def wide(value):
        return jnp.concatenate([value, value], axis=1)

    before = [[jnp.zeros((1, WIDTH), jnp.float32)] * 2]
    for b in range(blocks):
        acc = [jnp.zeros((8, WIDTH), jnp.float32)] * 2
        for low in range(0, TRI, SLAB):
            at = slice(b * TRI + low, b * TRI + low + SLAB)
            kr = wide(tables[0, at, :])
            for p in range(2):
                lanes = slice(p * WIDTH, (p + 1) * WIDTH)
                s = corr[p, at, :] + 0.25 * prev[p, at, :]
                section[p, at, :] = s
                u = s * kr
                high, rest = split(u)
                u_parts[b, low:low + SLAB, lanes] = high
                u_parts[b, TRI + low:TRI + low + SLAB, lanes] = rest
                high, rest = split(s * kc)
                for c in range(WIDTH // TRI):
                    beneath = slice(c * TRI, (c + 1) * TRI)
                    w_parts[b, c, p * TRI + low:p * TRI + low + SLAB, :TRI] = high[:, beneath]
                    w_parts[b, c, p * TRI + low:p * TRI + low + SLAB, TRI:] = rest[:, beneath]
                acc[p] = acc[p] + jnp.sum(u.reshape(SLAB // 8, 8, WIDTH), axis=0)
        left[b] = jnp.dot(lower2[...], u_parts[b], preferred_element_type=jnp.float32)
        for c in range(WIDTH // TRI):
            right[b, c] = jnp.dot(w_parts[b, c], upper2[...], preferred_element_type=jnp.float32)
        before.append([before[-1][p] + jnp.sum(acc[p], axis=0, keepdims=True) for p in range(2)])

    for b in range(blocks):
        for low in range(0, TRI, SLAB):
            at = slice(b * TRI + low, b * TRI + low + SLAB)
            ar, ai, pi, di = [wide(tables[t, at, :]) for t in range(1, 5)]
            s = [section[p, at, :] for p in range(2)]
            x = [left[b, low:low + SLAB, p * WIDTH:(p + 1) * WIDTH] for p in range(2)]
            if b:
                x = [x[p] + before[b][p] for p in range(2)]
            y = []
            for p in range(2):
                held = carry[p, at, :]
                near = slice(p * TRI + low, p * TRI + low + SLAB)
                pieces = []
                for c in range(WIDTH // TRI):
                    pieces.append(right[b, c, near, :TRI] + held)
                    held = held + right[b, c, near, TRI:]
                y.append(jnp.concatenate(pieces, axis=1))
                carry[p, at, :] = held
            cr = pi + pk
            ci = ak - di
            out[0, at, here] = (cr * s[0] - ci * s[1]) + (ar * x[0] - ai * x[1]) + (br * y[0] - bi * y[1])
            out[1, at, here] = (cr * s[1] + ci * s[0]) + (ar * x[1] + ai * x[0]) + (br * y[1] + bi * y[0])
    before = before[-1]

    offset = col_start - row_start

    @pl.when(jnp.logical_and(offset >= 0, offset < rows))
    def _():
        at = pl.ds(pl.multiple_of(offset, WIDTH), WIDTH)
        above = lax.broadcasted_iota(jnp.int32, (WIDTH, WIDTH), 0)
        beside = lax.broadcasted_iota(jnp.int32, (WIDTH, WIDTH), 1)
        out[0, at, here] += jnp.where(above == beside, wide(pump_col[at, :]), 0.0)

    sums[:, here] = jnp.concatenate(before, axis=0)

    @pl.when(step == pl.num_programs(0) - 1)
    def _():
        count, _, width = row_sums.shape
        for n in range(count):
            row_sums[n] = sums[:, n * width:(n + 1) * width]
        for p in range(2):
            col_sums[8 * p:8 * p + 8, :] = jnp.transpose(carry[p])[:8, :]


def prefix_pair(value, total, rho_re, rho_im):
    re = value[0:1] + rho_re * (total[0:1] - value[0:1]) - rho_im * (total[1:2] - value[1:2])
    im = value[1:2] + rho_re * (total[1:2] - value[1:2]) + rho_im * (total[0:1] - value[0:1])
    return re, im


def exchange_kernel(row_sums, col_sums, trip, row_fix, col_fix,
                    got, back, ready, cols_got, send, recv, send_back, recv_back, send_col, recv_col):
    count = row_sums.shape[0]
    col_count = cols_got.shape[0]
    me = lax.axis_index("row")
    my_col = lax.axis_index("col")
    rho_re = trip[0]
    rho_im = trip[1]

    def row_peer(j):
        return (lax.rem(me + j, count), my_col)

    def col_peer(j):
        return (me, lax.rem(my_col + j, col_count))

    barrier = pltpu.get_barrier_semaphore()
    for j in range(1, count):
        pl.semaphore_signal(barrier, inc=1, device_id=row_peer(j), device_id_type=MESH)
    for j in range(1, col_count):
        pl.semaphore_signal(barrier, inc=1, device_id=col_peer(j), device_id_type=MESH)
    pl.semaphore_wait(barrier, count + col_count - 2)

    first, second, across = [], [], []
    for j in range(1, count):
        first.append(pltpu.make_async_remote_copy(
            src_ref=row_sums.at[lax.rem(me + j, count)], dst_ref=got.at[j],
            send_sem=send.at[j], recv_sem=recv.at[j], device_id=row_peer(j), device_id_type=MESH))
        first[-1].start()
    for j in range(1, col_count):
        across.append(pltpu.make_async_remote_copy(
            src_ref=col_sums, dst_ref=cols_got.at[j],
            send_sem=send_col.at[j], recv_sem=recv_col.at[j], device_id=col_peer(j), device_id_type=MESH))
        across[-1].start()
    got[0] = row_sums[me]
    cols_got[0] = col_sums[...]
    for copy in first:
        copy.wait_recv()
    running = jnp.zeros(got.shape[1:], jnp.float32)
    held = []
    for n in range(count):
        held.append(running)
        running = running + got[lax.rem(me - n + count, count)]
    for n in range(count):
        re, im = prefix_pair(held[n], running, rho_re, rho_im)
        ready[lax.rem(n - me + count, count)] = jnp.concatenate([re, im], axis=0)
    for j in range(1, count):
        second.append(pltpu.make_async_remote_copy(
            src_ref=ready.at[j], dst_ref=back.at[j],
            send_sem=send_back.at[j], recv_sem=recv_back.at[j], device_id=row_peer(j), device_id_type=MESH))
        second[-1].start()
    for copy in across:
        copy.wait_recv()
    running = jnp.zeros(col_sums.shape, jnp.float32)
    mine = running
    for n in range(col_count):
        piece = cols_got[lax.rem(my_col - n + col_count, col_count)]
        mine = mine + jnp.where(n < my_col, piece, 0.0)
        running = running + piece
    rest = running - mine
    col_fix[0:8, :] = mine[0:8] + rho_re * rest[0:8] + rho_im * rest[8:16]
    col_fix[8:16, :] = mine[8:16] + rho_re * rest[8:16] - rho_im * rest[0:8]
    for copy in second:
        copy.wait_recv()
    row_fix[me] = ready[0]
    for j in range(1, count):
        row_fix[lax.rem(me - j + count, count)] = back[j]
    for copy in first + across + second:
        copy.wait_send()


def finish_kernel(local, row_fix, col_fix, kappa, out, tables, across):
    step = pl.program_id(0)
    rows = local.shape[1]
    cols = local.shape[2]
    slab = out.shape[1]

    @pl.when(step == 0)
    def _():
        mine = pl.ds(pl.multiple_of(lax.axis_index("row") * rows, WIDTH), rows)
        stacked = jnp.concatenate([col_fix[0:1, :], col_fix[8:9, :], kappa[:, mine]] + [col_fix[0:5, :]], axis=0)
        columns = jnp.transpose(stacked)
        for n in range(3):
            tables[n] = jnp.broadcast_to(columns[:, n:n + 1], tables.shape[1:])
        count = row_fix.shape[0]
        across[...] = jnp.concatenate([row_fix[n] for n in range(count)], axis=1)

    at = pl.ds(pl.multiple_of(step * slab, slab), slab)
    col_start = lax.axis_index("col") * cols
    kr = tables[2, at, :]
    fix = [tables[p, at, :] for p in range(2)]
    for n in range(cols // 128):
        here = slice(n * 128, (n + 1) * 128)
        kc = kappa[:, pl.ds(pl.multiple_of(col_start + n * 128, 128), 128)]
        for p in range(2):
            out[p, :, here] = local[p, at, here] - kr * across[p:p + 1, here] - kc * fix[p]


def shards(row_count, col_count, corr, slope_prev, kappa, detuning, pump, round_trip):
    _, rows, cols = corr.shape
    width = cols // row_count
    kappa, detuning, pump = [v.reshape(1, -1) for v in (kappa, detuning, pump)]
    f32 = jnp.float32
    block = pl.BlockSpec((2, rows, WIDTH), lambda c: (0, 0, c))
    local, row_sums, col_sums = pl.pallas_call(
        local_kernel,
        grid=(cols // WIDTH,),
        out_shape=(
            pltpu.VMEM((2, rows, cols), f32),
            jax.ShapeDtypeStruct((row_count, 2, width), f32),
            jax.ShapeDtypeStruct((16, rows), f32),
        ),
        in_specs=[block, block, VMEM, VMEM, VMEM, SMEM],
        out_specs=(VMEM, VMEM, VMEM),
        scratch_shapes=[
            pltpu.VMEM((5, rows, WIDTH // 2), f32),
            pltpu.VMEM((rows, WIDTH // 2), f32),
            pltpu.VMEM((rows // TRI, 2 * TRI, 2 * WIDTH), jnp.bfloat16),
            pltpu.VMEM((rows // TRI, WIDTH // TRI, 2 * TRI, 2 * TRI), jnp.bfloat16),
            pltpu.VMEM((rows // TRI, TRI, 2 * WIDTH), f32),
            pltpu.VMEM((rows // TRI, WIDTH // TRI, 2 * TRI, 2 * TRI), f32),
            pltpu.VMEM((2, rows, WIDTH // 2), f32),
            pltpu.VMEM((2, cols), f32),
            pltpu.VMEM((TRI, 2 * TRI), jnp.bfloat16),
            pltpu.VMEM((2 * TRI, 2 * TRI), jnp.bfloat16),
            pltpu.VMEM((2, rows, WIDTH), f32),
        ],
        compiler_params=pltpu.CompilerParams(vmem_limit_bytes=34 << 20),
        name="local_part",
    )(corr, slope_prev, kappa, detuning, pump, round_trip)
    piece = (row_count, 2, width)
    row_fix, col_fix = pl.pallas_call(
        exchange_kernel,
        out_shape=(jax.ShapeDtypeStruct(piece, f32), jax.ShapeDtypeStruct((16, rows), f32)),
        in_specs=[VMEM, VMEM, SMEM],
        out_specs=(VMEM, VMEM),
        scratch_shapes=[
            pltpu.VMEM(piece, f32),
            pltpu.VMEM(piece, f32),
            pltpu.VMEM(piece, f32),
            pltpu.VMEM((col_count, 16, rows), f32),
        ] + [pltpu.SemaphoreType.DMA((row_count,))] * 4 + [pltpu.SemaphoreType.DMA((col_count,))] * 2,
        compiler_params=pltpu.CompilerParams(
            collective_id=0, has_side_effects=True, vmem_limit_bytes=6 << 20),
        name="exchange_sums",
    )(row_sums, col_sums, round_trip)
    slab = 32
    return pl.pallas_call(
        finish_kernel,
        grid=(rows // slab,),
        out_shape=jax.ShapeDtypeStruct((2, rows, cols), f32),
        in_specs=[VMEM, VMEM, VMEM, VMEM],
        out_specs=pl.BlockSpec((2, slab, cols), lambda r: (0, r, 0)),
        scratch_shapes=[pltpu.VMEM((3, rows, 128), f32), pltpu.VMEM((2, cols), f32)],
        compiler_params=pltpu.CompilerParams(vmem_limit_bytes=10 << 20),
        name="finish",
    )(local, row_fix, col_fix, kappa)


def solution(mesh):
    placed = (P(None, "row", "col"), P(None, "row", "col"), P(), P(), P(), P())
    body = functools.partial(shards, mesh.shape["row"], mesh.shape["col"])
    return jax.shard_map(
        body, mesh=mesh, in_specs=placed, out_specs=P(None, "row", "col"), check_vma=False
    )
```
